512 devices in a mesh: vpair: 64 (over y_hi, z, x), occ: 8 (over y_lo, core).
Axes of the slice: x: 4, y: 8 (y_hi: 2, y_lo: 4; y = y_hi * 4 + y_lo), z: 8, core: 2. Of those that a mesh axis runs over, the one named last changes fastest.
Arguments:
- amplitudes: bfloat16 [64, 256, 128, 128], P('vpair', 'occ'), may hold values from -6 to 6
- fock_blocks: bfloat16 [8, 128, 128], replicated, may hold values from -0.5 to 0.5
- owner_map: int32 [64, 2], replicated, may hold values from 0 to 7, as said below
- extents: int32 [8], replicated, may hold values from 64 to 128
Outputs:
- doubles: bfloat16 [64, 256, 128, 128], P('vpair', 'occ')
The draws below stay inside these ranges and needn't reach their ends.
Inputs may be any that keep to these rules, and one draw needn't show every extreme that they name: `owner_map`: rows s and s + 32 name mirrored blocks (A, B) and (B, A), or each names a diagonal pair (A, A); every ordered pair of blocks stands in exactly one row.
All inputs are finite; a program needn't handle non-finite values.
Results may differ from the reference program's by a relative error of at most 0.0079.
Values may be sent and summed in bfloat16 or wider, within the bound.
A program may use at most 64 MiB of HBM per device.

```python
import math
import jax
import jax.numpy as jnp
import numpy as np
from jax import lax

NB = 8
BLK = 128
VIRT = 1024
NPAIR = 64
OCC_PAIRS = 256


def draw_owner_map(key, part):
    key = jax.random.fold_in(key, 11)
    key_order, key_flip, key_label = jax.random.split(key, 3)
    leading_list = []
    trailing_list = []
    for block_one in range(NB):
        for block_two in range(block_one + 1, NB):
            leading_list.append((block_one, block_two))
            trailing_list.append((block_two, block_one))
    for couple in range(NB // 2):
        leading_list.append((2 * couple, 2 * couple))
        trailing_list.append((2 * couple + 1, 2 * couple + 1))
    leading_tab = jnp.asarray(np.array(leading_list, dtype=np.int32))
    trailing_tab = jnp.asarray(np.array(trailing_list, dtype=np.int32))
    order = jax.random.permutation(key_order, NPAIR // 2)
    flipped = jax.random.randint(key_flip, (NPAIR // 2, 1), 0, 2)
    chosen_lead = leading_tab[order]
    chosen_trail = trailing_tab[order]
    lower_half = jnp.where(flipped == 1, chosen_trail, chosen_lead)
    upper_half = jnp.where(flipped == 1, chosen_lead, chosen_trail)
    table = jnp.concatenate([lower_half, upper_half], axis=0)
    relabel = jax.random.permutation(key_label, NB).astype(jnp.int32)
    return relabel[table].astype(jnp.int32)


def draw_extents(key, part):
    key = jax.random.fold_in(key, 23)
    key_vals, key_top, key_off = jax.random.split(key, 3)
    values = jax.random.randint(key_vals, (NB,), BLK // 2, BLK + 1)
    largest = jax.random.randint(key_top, (), 0, NB)
    offset = jax.random.randint(key_off, (), 1, NB)
    smallest = (largest + offset) % NB
    values = values.at[largest].set(BLK).at[smallest].set(BLK // 2)
    return values.astype(jnp.int32)


def block_levels(own_key, shape, shards, low, high):
    factor_of, own = 1.0, jax.random.fold_in(own_key, 6)
    for axis_at, shards_of in shards:
        heights = jnp.exp(jax.random.uniform(jax.random.fold_in(own, axis_at), (shards_of,), jnp.float32, low / len(shards), high / len(shards)))
        factor_of = factor_of * jnp.repeat(heights, shape[axis_at] // shards_of).reshape([-1 if axis == axis_at else 1 for axis in range(len(shape))])
    return factor_of


def noise(stream_key, shape, width, limit, cuts=(), kind=jnp.bfloat16):
    values = jax.random.normal(stream_key, shape, jnp.float32) * width
    if len(cuts) > 0:
        values = block_levels(stream_key, shape, cuts, -0.22, 0.18) * values
    return jnp.clip(values, min=-limit, max=limit).astype(kind)


def setup_inputs(seed: int = 0) -> dict:
    seeds = jax.random.split(jax.random.key(seed), 5)
    amplitudes = noise(seeds[0], (NPAIR, OCC_PAIRS, BLK, BLK), 1.0, 6.0, ((0, 64), (1, 8)))
    fock_blocks = noise(seeds[1], (NB, BLK, BLK), BLK ** -0.5, 0.5)
    owner_map = draw_owner_map(jax.random.fold_in(seeds[4], 71), 0)
    extents = draw_extents(jax.random.fold_in(seeds[4], 71), 0)
    return {"amplitudes": amplitudes, "fock_blocks": fock_blocks, "owner_map": owner_map, "extents": extents}


def reference(amplitudes, fock_blocks, owner_map, extents):
    half_pairs = NPAIR // 2
    orbital = jnp.arange(BLK, dtype=jnp.int32)

    def antisym(slot):
        own_tile = amplitudes[slot]
        other = amplitudes[(slot + half_pairs) % NPAIR]
        block_a = owner_map[slot, 0]
        block_b = owner_map[slot, 1]
        other = jnp.where(block_a == block_b, own_tile, other)
        live = (orbital[:, None] < extents[block_a]) & (orbital[None, :] < extents[block_b])
        diff = own_tile.astype(jnp.float32) - jnp.swapaxes(other, 1, 2).astype(jnp.float32)
        return jnp.where(live[None], diff, jnp.float32(0.0)).astype(jnp.bfloat16)
    anti = lax.map(antisym, jnp.arange(NPAIR, dtype=jnp.int32))

    def accumulate(summed, slot):
        tiles = anti[slot].astype(jnp.float32)
        fock_a = fock_blocks[owner_map[slot, 0]].astype(jnp.float32)
        fock_b = fock_blocks[owner_map[slot, 1]].astype(jnp.float32)
        half_image = jnp.einsum('ji,qjb->qib', fock_a, tiles).astype(jnp.bfloat16)
        half_image = lax.optimization_barrier(half_image).astype(jnp.float32)
        image = jnp.einsum('qib,bc->qic', half_image, fock_b).astype(jnp.bfloat16)
        image = lax.optimization_barrier(image).astype(jnp.float32)
        return (summed + jnp.einsum('pab,qab->pq', tiles, image), None)
    summed, _ = lax.scan(accumulate, jnp.zeros((OCC_PAIRS, OCC_PAIRS), jnp.float32), jnp.arange(NPAIR, dtype=jnp.int32))
    intersection = (summed / float(VIRT)).astype(jnp.bfloat16)
    intersection = lax.optimization_barrier(intersection).astype(jnp.float32)
    factor = 1.0 / math.sqrt(OCC_PAIRS)

    def residual(slot):
        term = jnp.einsum('pq,qab->pab', intersection, anti[slot].astype(jnp.float32))
        return (term * factor).astype(jnp.bfloat16)
    return lax.map(residual, jnp.arange(NPAIR, dtype=jnp.int32))
```

```python
import functools
import math

import jax
import jax.numpy as jnp
from jax import lax
from jax.experimental import pallas as pl
from jax.experimental.pallas import tpu as pltpu
from jax.sharding import PartitionSpec as P

MESH = pl.DeviceIdType.MESH
CHUNKS = 4
NT = (((1,), (1,)), ((), ()))
NN = (((1,), (0,)), ((), ()))


def dot(left, right, dims):
    return lax.dot_general(left, right, dims, preferred_element_type=jnp.float32)


def kernel(
    sizes,
    amps, fock, owner, extents, out,
    own, received, fk, xf, yf, yb, tiles, acc, part_x, part_z, rows_own, rows_other, zs, packed_out,
    load_sem, ex_send, ex_recv, up_send, up_recv, down_send, down_recv,
    core_send, core_recv, x_send, x_recv, z_send, z_recv, swap_send, swap_recv, out_sem,
):
    ring, nz, nx = sizes
    half = ring // 2
    per_side = ring // 2
    plane = nz * nx
    mine, width = own.shape[0], own.shape[1]
    both = 2 * mine
    group = mine // CHUNKS
    span = width // CHUNKS

    v = lax.axis_index("vpair")
    o = lax.axis_index("occ")
    side = lax.div(v, plane)
    w = lax.rem(v, plane)
    z = lax.div(w, nx)
    x = lax.rem(w, nx)
    core = lax.rem(o, 2)
    y = side * per_side + lax.div(o, 2)

    def device(y_at, core_at, w_at):
        return (
            lax.div(y_at, per_side) * plane + w_at,
            lax.rem(y_at, per_side) * 2 + core_at,
        )

    mirror = device(lax.rem(y + half, ring), core, w)
    above = device(lax.rem(y + 1, ring), core, w)
    below = device(lax.rem(y + ring - 1, ring), core, w)
    sibling = device(y, 1 - core, w)
    x_at = [lax.rem(x + d, nx) for d in range(nx)]
    z_at = [lax.rem(z + d, nz) for d in range(nz)]
    x_peer = [device(y, core, z * nx + at) for at in x_at]
    z_peer = [device(y, core, at * nx + x) for at in z_at]

    loads = [
        pltpu.make_async_copy(
            amps.at[0, pl.ds(side * mine, mine)], own, load_sem.at[0]
        ),
        pltpu.make_async_copy(fock, fk, load_sem.at[1]),
    ]
    for copy in loads:
        copy.start()

    peers = [mirror, above, below, sibling] + x_peer[1:] + z_peer[1:]
    barrier = pltpu.get_barrier_semaphore()
    for peer in peers:
        pl.semaphore_signal(barrier, inc=1, device_id=peer, device_id_type=MESH)
    pl.semaphore_wait(barrier, len(peers))

    def remote(src, dst, send, recv, to):
        return pltpu.make_async_remote_copy(
            src_ref=src, dst_ref=dst, send_sem=send, recv_sem=recv,
            device_id=to, device_id_type=MESH,
        )

    def exchange(c):
        return remote(
            amps.at[0, pl.ds((1 - side) * mine + c * group, group)],
            received.at[pl.ds(c * group, group)],
            ex_send.at[c], ex_recv.at[c], mirror,
        )

    for c in range(CHUNKS):
        exchange(c).start()

    lower_slot = w
    upper_slot = w + plane
    a_low, b_low = owner[lower_slot, 0], owner[lower_slot, 1]
    a_high, b_high = owner[upper_slot, 0], owner[upper_slot, 1]
    off = (a_low != b_low).astype(jnp.int32)
    is_low = 1 - side
    row = lax.broadcasted_iota(jnp.int32, (width, width), 0)
    col = lax.broadcasted_iota(jnp.int32, (width, width), 1)
    above_diag = jnp.where(row < col, 1, 0)
    below_diag = jnp.where(row > col, 1, 0)
    first_i = jnp.minimum(above_diag + off, 1)
    second_i = below_diag * (1 - off)
    first = first_i > 0
    live = (row < jnp.where(first, extents[a_low], extents[a_high])) & (
        col < jnp.where(first, extents[b_low], extents[b_high])
    )
    plus_own = first_i == is_low
    minus_own = second_i == is_low

    for copy in loads:
        copy.wait()
    fock_a1, fock_b1 = fk[a_low], fk[b_low]
    fock_a2, fock_b2 = fk[a_high], fk[b_high]

    acc[...] = jnp.zeros_like(acc)

    def build(p, carry):
        mine_t = own[p].astype(jnp.float32)
        other_t = received[p].astype(jnp.float32)
        plus = jnp.where(plus_own, mine_t, other_t)
        minus = jnp.where(minus_own, mine_t, other_t)
        tile = jnp.where(live, plus - minus.T, 0.0).astype(jnp.bfloat16)
        tile = tile.astype(jnp.float32)
        turned = -tile.T
        one = jnp.where(first, tile, turned).astype(jnp.bfloat16)
        two = jnp.where(below_diag > 0, tile, turned).astype(jnp.bfloat16)
        half_one = dot(one, fock_b1, NT).astype(jnp.bfloat16)
        half_two = dot(two, fock_b2, NT).astype(jnp.bfloat16)
        image = jnp.where(
            first, dot(fock_a1, half_one, NN), dot(fock_a2, half_two, NN)
        )
        xf[pl.ds(p, width, stride=mine), :] = tile
        yf[pl.ds(p, width, stride=mine), :] = image
        return carry

    for c in range(CHUNKS):
        exchange(c).wait_recv()
        lax.fori_loop(c * group, (c + 1) * group, build, 0)

    def up(t, c):
        at = lax.rem(ring - t, ring) if not isinstance(t, int) else (ring - t) % ring
        return remote(
            tiles.at[at, 0, pl.ds(c * span, span)],
            tiles.at[ring - 1 - t, 0, pl.ds(c * span, span)],
            up_send.at[t, c], up_recv.at[t, c], above,
        )

    def down(t, c):
        return remote(
            tiles.at[t, 0, pl.ds(c * span, span)],
            tiles.at[t + 1, 0, pl.ds(c * span, span)],
            down_send.at[t, c], down_recv.at[t, c], below,
        )

    def across(r, c):
        return remote(
            tiles.at[r, 0, pl.ds(c * span, span)],
            tiles.at[r, 1, pl.ds(c * span, span)],
            core_send.at[r, c], core_recv.at[r, c], sibling,
        )

    for c in range(CHUNKS):
        block = xf[pl.ds(c * span * mine, span * mine), :].astype(jnp.bfloat16)
        tiles[0, 0, pl.ds(c * span, span)] = block.reshape(span, mine, width)
        up(0, c).start()
        down(0, c).start()
        across(0, c).start()
    for c in range(CHUNKS):
        block = yf[pl.ds(c * span * mine, span * mine), :].astype(jnp.bfloat16)
        yb[pl.ds(c * span, span)] = block.reshape(span, mine, width)

    unroll = min(8, span)

    def contract(slots, c):
        def some(i, sums):
            lefts, rights = [], []
            for u in range(unroll):
                a = c * span + i * unroll + u
                rights.append(yb[a])
                lefts.append(
                    jnp.concatenate([tiles[r, k, a] for r in slots for k in (0, 1)], 0)
                )
            return sums + dot(
                jnp.concatenate(lefts, 1), jnp.concatenate(rights, 1), NT
            )

        start = jnp.zeros((len(slots) * both, mine), jnp.float32)
        sums = lax.fori_loop(0, span // unroll, some, start)
        for n, r in enumerate(slots):
            acc[pl.ds(r * both, both), pl.ds(0, mine)] += sums[n * both : (n + 1) * both]

    def slots_at(t):
        return [t] if t in (0, half) else [t, ring - t]

    for t in range(half):
        for c in range(CHUNKS):
            up_here = t < half - 1 or c < CHUNKS // 2
            down_here = t < half - 1 or c >= CHUNKS // 2
            if up_here:
                up(t, c).wait_recv()
                if t + 1 < half - 1 or (t + 1 == half - 1 and c < CHUNKS // 2):
                    up(t + 1, c).start()
                across(ring - 1 - t, c).start()
            if down_here:
                down(t, c).wait_recv()
                if t + 1 < half - 1 or (t + 1 == half - 1 and c >= CHUNKS // 2):
                    down(t + 1, c).start()
                across(t + 1, c).start()
            for r in slots_at(t):
                across(r, c).wait_recv()
            contract(slots_at(t), c)
    for c in range(CHUNKS):
        across(half, c).wait_recv()
        contract([half], c)

    rows = ring * both
    turned = jnp.concatenate(
        [acc[pl.ds(n * width, width), :].T[:mine] for n in range(rows // width)], 1
    )
    part_x[x] = turned
    def send_x(d):
        return remote(part_x.at[x], part_x.at[x], x_send.at[d], x_recv.at[x], x_peer[d])

    def wait_x(d):
        return remote(
            part_x.at[x_at[d]], part_x.at[x_at[d]], x_send.at[d], x_recv.at[x_at[d]], x_peer[d]
        )

    def send_z(d):
        return remote(part_z.at[z], part_z.at[z], z_send.at[d], z_recv.at[z], z_peer[d])

    def wait_z(d):
        return remote(
            part_z.at[z_at[d]], part_z.at[z_at[d]], z_send.at[d], z_recv.at[z_at[d]], z_peer[d]
        )

    for d in range(1, nx):
        send_x(d).start()
    for d in range(1, nx):
        wait_x(d).wait_recv()
    total = part_x[0]
    for n in range(1, nx):
        total += part_x[n]
    part_z[z] = total
    for d in range(1, nz):
        send_z(d).start()
    for d in range(1, nz):
        wait_z(d).wait_recv()
    total = part_z[0]
    for n in range(1, nz):
        total += part_z[n]

    nblocks = fk.shape[0]
    rows_own[...] = (total * (2.0 / (nblocks * width))).astype(jnp.bfloat16)
    swap = remote(rows_own, rows_other, swap_send.at[0], swap_recv.at[0], mirror)
    swap.start()
    swap.wait_recv()
    here = rows_own[...].astype(jnp.float32)
    there = rows_other[...].astype(jnp.float32)
    cut = half * both
    there = jnp.concatenate([there[:, cut:], there[:, :cut]], 1)
    low = jnp.zeros(here.shape, jnp.int32) + side == 0
    inter = jnp.concatenate(
        [jnp.where(low, here, there), jnp.where(low, there, here)], 0
    ).astype(jnp.bfloat16)
    factor = 1.0 / math.sqrt(rows)

    pair = 2

    def residual(i, carry):
        a = i * pair
        right = jnp.concatenate(
            [tiles[:, :, a + u].reshape(rows, width) for u in range(pair)], 1
        )
        made = dot(inter, right, NN) * factor
        for u in range(pair):
            zs[pl.ds((a + u) * both, both), :] = made[:, u * width : (u + 1) * width]
        return carry

    lax.fori_loop(0, width // pair, residual, 0)

    triangle = is_low * above_diag + side * below_diag
    keep = (off * is_low + (1 - off) * triangle) > 0

    def unpack(p, carry):
        tile = zs[pl.ds(p, width, stride=both), :]
        packed_out[p] = jnp.where(keep, tile, -tile.T).astype(jnp.bfloat16)
        return carry

    def write(c):
        size = both // CHUNKS
        return pltpu.make_async_copy(
            packed_out.at[pl.ds(c * size, size)], out.at[0, pl.ds(c * size, size)], out_sem.at[c]
        )

    for c in range(CHUNKS):
        size = both // CHUNKS
        lax.fori_loop(c * size, (c + 1) * size, unpack, 0)
        write(c).start()

    for c in range(CHUNKS):
        exchange(c).wait_send()
        for t in range(half):
            if t < half - 1 or c < CHUNKS // 2:
                up(t, c).wait_send()
            if t < half - 1 or c >= CHUNKS // 2:
                down(t, c).wait_send()
        for r in range(ring):
            across(r, c).wait_send()
    for d in range(1, nx):
        send_x(d).wait_send()
    for d in range(1, nz):
        send_z(d).wait_send()
    swap.wait_send()
    for c in range(CHUNKS):
        write(c).wait()


def body(sizes, amplitudes, fock_blocks, owner_map, extents):
    ring, nz, nx = sizes
    slots, both, width = amplitudes.shape[0], amplitudes.shape[1], amplitudes.shape[2]
    mine = both // 2
    half = ring // 2
    rows = ring * both
    dma = pltpu.SemaphoreType.DMA
    any_space = pl.BlockSpec(memory_space=pl.ANY)
    smem = pl.BlockSpec(memory_space=pltpu.SMEM)
    bf16, f32 = jnp.bfloat16, jnp.float32
    return pl.pallas_call(
        functools.partial(kernel, sizes),
        out_shape=jax.ShapeDtypeStruct((slots, both, width, width), bf16),
        in_specs=[any_space, any_space, smem, smem],
        out_specs=any_space,
        scratch_shapes=[
            pltpu.VMEM((mine, width, width), bf16),
            pltpu.VMEM((mine, width, width), bf16),
            pltpu.VMEM(fock_blocks.shape, bf16),
            pltpu.VMEM((width * mine, width), f32),
            pltpu.VMEM((width * mine, width), f32),
            pltpu.VMEM((width, mine, width), bf16),
            pltpu.VMEM((ring, 2, width, mine, width), bf16),
            pltpu.VMEM((rows, width), f32),
            pltpu.VMEM((nx, mine, rows), f32),
            pltpu.VMEM((nz, mine, rows), f32),
            pltpu.VMEM((mine, rows), bf16),
            pltpu.VMEM((mine, rows), bf16),
            pltpu.VMEM((width * both, width), f32),
            pltpu.VMEM((both, width, width), bf16),
            dma((2,)),
            dma((CHUNKS,)), dma((CHUNKS,)),
            dma((half, CHUNKS)), dma((half, CHUNKS)),
            dma((half, CHUNKS)), dma((half, CHUNKS)),
            dma((ring, CHUNKS)), dma((ring, CHUNKS)),
            dma((nx,)), dma((nx,)),
            dma((nz,)), dma((nz,)),
            dma((1,)), dma((1,)),
            dma((CHUNKS,)),
        ],
        compiler_params=pltpu.CompilerParams(
            collective_id=0, has_side_effects=True, vmem_limit_bytes=48 * 1024 * 1024
        ),
        cost_estimate=pl.CostEstimate(
            flops=2**30, bytes_accessed=2**22, transcendentals=0
        ),
    )(amplitudes, fock_blocks, owner_map, extents)


def solution(mesh):
    plane = mesh.shape["vpair"] // 2
    nx = 4 if plane % 4 == 0 else 1
    sizes = (mesh.shape["occ"], plane // nx, nx)
    placed = (P("vpair", "occ", None, None), P(), P(), P())
    return jax.shard_map(
        functools.partial(body, sizes),
        mesh=mesh,
        in_specs=placed,
        out_specs=P("vpair", "occ", None, None),
        check_vma=False,
    )
```

```python
import functools
import math

import jax
import jax.numpy as jnp
from jax import lax
from jax.experimental import pallas as pl
from jax.experimental.pallas import tpu as pltpu
from jax.sharding import PartitionSpec as P

MESH = pl.DeviceIdType.MESH
CHUNKS = 4
DEPTH = 4
NT = (((1,), (1,)), ((), ()))
NN = (((1,), (0,)), ((), ()))


def dot(left, right, dims):
    return lax.dot_general(left, right, dims, preferred_element_type=jnp.float32)


def kernel(
    sizes,
    amps, fock, owner_at, extents_at, out,
    owner, extents, own, received, fk, xf, yf, yb, tiles, acc, part_x, part_z, row_parts, zs,
    load_sem, ex_send, ex_recv, up_send, up_recv, down_send, down_recv,
    core_send, core_recv, x_send, x_recv, z_send, z_recv, row_send, row_recv,
):
    ring, nz, nx = sizes
    half = ring // 2
    per_side = ring // 2
    plane = nz * nx
    mine, width = own.shape[0], own.shape[1]
    both = 2 * mine
    group = mine // CHUNKS
    span = width // CHUNKS

    v = lax.axis_index("vpair")
    o = lax.axis_index("occ")
    side = lax.div(v, plane)
    w = lax.rem(v, plane)
    z = lax.div(w, nx)
    x = lax.rem(w, nx)
    core = lax.rem(o, 2)
    y = side * per_side + lax.div(o, 2)

    def device(y_at, core_at, w_at):
        return (
            lax.div(y_at, per_side) * plane + w_at,
            lax.rem(y_at, per_side) * 2 + core_at,
        )

    around = [device(lax.rem(y + d, ring), core, w) for d in range(ring)]
    mirror, above, below = around[half], around[1], around[ring - 1]
    sibling = device(y, 1 - core, w)
    x_at = [lax.rem(x + d, nx) for d in range(nx)]
    z_at = [lax.rem(z + d, nz) for d in range(nz)]
    x_peer = [device(y, core, z * nx + at) for at in x_at]
    z_peer = [device(y, core, at * nx + x) for at in z_at]

    loads = [
        pltpu.make_async_copy(
            amps.at[0, pl.ds(side * mine, mine)], own, load_sem.at[0]
        ),
        pltpu.make_async_copy(fock, fk, load_sem.at[1]),
        pltpu.make_async_copy(owner_at, owner, load_sem.at[2]),
        pltpu.make_async_copy(extents_at, extents, load_sem.at[3]),
    ]
    for copy in loads:
        copy.start()

    peers = around[1:] + [sibling] + x_peer[1:] + z_peer[1:]
    barrier = pltpu.get_barrier_semaphore()
    for peer in peers:
        pl.semaphore_signal(barrier, inc=1, device_id=peer, device_id_type=MESH)
    pl.semaphore_wait(barrier, len(peers))

    def remote(src, dst, send, recv, to):
        return pltpu.make_async_remote_copy(
            src_ref=src, dst_ref=dst, send_sem=send, recv_sem=recv,
            device_id=to, device_id_type=MESH,
        )

    def exchange(c):
        return remote(
            amps.at[0, pl.ds((1 - side) * mine + c * group, group)],
            received.at[pl.ds(c * group, group)],
            ex_send.at[c], ex_recv.at[c], mirror,
        )

    for c in range(CHUNKS):
        exchange(c).start()

    for copy in loads:
        copy.wait()

    lower_slot = w
    upper_slot = w + plane
    a_low, b_low = owner[0, lower_slot], owner[1, lower_slot]
    a_high, b_high = owner[0, upper_slot], owner[1, upper_slot]
    off = (a_low != b_low).astype(jnp.int32)
    is_low = 1 - side
    row = lax.broadcasted_iota(jnp.int32, (width, width), 0)
    col = lax.broadcasted_iota(jnp.int32, (width, width), 1)
    above_diag = jnp.where(row < col, 1, 0)
    below_diag = jnp.where(row > col, 1, 0)
    first_i = jnp.minimum(above_diag + off, 1)
    second_i = below_diag * (1 - off)
    first = first_i > 0
    live = (row < jnp.where(first, extents[a_low], extents[a_high])) & (
        col < jnp.where(first, extents[b_low], extents[b_high])
    )
    plus_own = first_i == is_low
    minus_own = second_i == is_low

    fock_a1, fock_b1 = fk[a_low], fk[b_low]
    fock_a2, fock_b2 = fk[a_high], fk[b_high]

    acc[...] = jnp.zeros_like(acc)

    def transform_tile(p, tile):
        turned = -tile.T
        one = jnp.where(first, tile, turned).astype(jnp.bfloat16)
        two = jnp.where(below_diag > 0, tile, turned).astype(jnp.bfloat16)
        half_one = dot(one, fock_b1, NT).astype(jnp.bfloat16)
        half_two = dot(two, fock_b2, NT).astype(jnp.bfloat16)
        yf[pl.ds(p, width, stride=mine), :] = jnp.where(
            first, dot(fock_a1, half_one, NN), dot(fock_a2, half_two, NN)
        )

    def build(p, carry):
        mine_t = own[p].astype(jnp.float32)
        other_t = received[p].astype(jnp.float32)
        plus = jnp.where(plus_own, mine_t, other_t)
        minus = jnp.where(minus_own, mine_t, other_t)
        tile = jnp.where(live, plus - minus.T, 0.0).astype(jnp.bfloat16)
        tile = tile.astype(jnp.float32)
        xf[pl.ds(p, width, stride=mine), :] = tile
        transform_tile(p, tile)
        return carry

    def transform(p, carry):
        transform_tile(p, xf[pl.ds(p, width, stride=mine), :])
        return carry

    for c in range(CHUNKS):
        exchange(c).wait_recv()
        lax.fori_loop(c * group, (c + 1) * group, build, 0, unroll=4)

    def up(t, c):
        at = lax.rem(ring - t, ring) if not isinstance(t, int) else (ring - t) % ring
        return remote(
            tiles.at[at, 0, pl.ds(c * span, span)],
            tiles.at[ring - 1 - t, 0, pl.ds(c * span, span)],
            up_send.at[t, c], up_recv.at[t, c], above,
        )

    def down(t, c):
        return remote(
            tiles.at[t, 0, pl.ds(c * span, span)],
            tiles.at[t + 1, 0, pl.ds(c * span, span)],
            down_send.at[t, c], down_recv.at[t, c], below,
        )

    def across(r, c):
        return remote(
            tiles.at[r, 0, pl.ds(c * span, span)],
            tiles.at[r, 1, pl.ds(c * span, span)],
            core_send.at[r, c], core_recv.at[r, c], sibling,
        )

    middle = CHUNKS // 2
    up_order = list(range(CHUNKS))
    down_order = up_order[middle:] + up_order[:middle]
    up_steps = [(t, c) for t in range(half) for c in up_order][: -middle]
    down_steps = [(t, c) for t in range(half) for c in down_order][: -middle]

    def start(i):
        if i < len(up_steps):
            up(*up_steps[i]).start()
            down(*down_steps[i]).start()

    def own_chunk(c):
        block = xf[pl.ds(c * span * mine, span * mine), :].astype(jnp.bfloat16)
        tiles[0, 0, pl.ds(c * span, span)] = block.reshape(span, mine, width)

    for i in range(CHUNKS):
        if i < middle:
            own_chunk(up_order[i])
            own_chunk(down_order[i])
        start(i)
    for c in range(CHUNKS):
        across(0, c).start()

    def image_done(n):
        def some(c, carry):
            block = yf[pl.ds(c * span * mine, span * mine), :].astype(jnp.bfloat16)
            yb[n, pl.ds(c * span, span)] = block.reshape(span, mine, width)
            return carry

        lax.fori_loop(0, CHUNKS, some, 0)

    def block_in(r):
        def some(c, carry):
            block = tiles[r, 0, pl.ds(c * span, span)].reshape(span * mine, width)
            xf[pl.ds(c * span * mine, span * mine), :] = block.astype(jnp.float32)
            return carry

        lax.fori_loop(0, CHUNKS, some, 0)

    image_done(0)
    unroll = min(32, span)

    def contract(n, slots, to, begin, count):
        def some(i, sums):
            lefts, rights = [], []
            for u in range(unroll):
                a = begin + i * unroll + u
                rights.append(yb[n, a])
                lefts.append(
                    jnp.concatenate([tiles[r, k, a] for r in slots for k in (0, 1)], 0)
                )
            return sums + dot(
                jnp.concatenate(lefts, 1), jnp.concatenate(rights, 1), NT
            )

        zero = jnp.zeros((len(slots) * both, mine), jnp.float32)
        sums = lax.fori_loop(0, count // unroll, some, zero, unroll=min(4, count // unroll))
        for m, r in enumerate(to):
            acc[pl.ds(r * both, both), pl.ds(0, mine)] += sums[m * both : (m + 1) * both]

    def receive(i):
        t, c = up_steps[i]
        up(t, c).wait_recv()
        up(t, c).wait_send()
        across(ring - 1 - t, c).start()
        t, c = down_steps[i]
        down(t, c).wait_recv()
        down(t, c).wait_send()
        across(t + 1, c).start()
        start(i + DEPTH)

    def arrived(r, c):
        across(r, c).wait_recv()

    def send_x(d):
        return remote(part_x.at[x], part_x.at[x], x_send.at[d], x_recv.at[x], x_peer[d])

    def wait_x(d):
        return remote(
            part_x.at[x_at[d]], part_x.at[x_at[d]], x_send.at[d], x_recv.at[x_at[d]], x_peer[d]
        )

    def send_z(d):
        return remote(part_z.at[z], part_z.at[z], z_send.at[d], z_recv.at[z], z_peer[d])

    def wait_z(d):
        return remote(
            part_z.at[z_at[d]], part_z.at[z_at[d]], z_send.at[d], z_recv.at[z_at[d]], z_peer[d]
        )

    def send_rows(d):
        return remote(
            row_parts[0], row_parts[ring - d], row_send.at[d], row_recv.at[ring - d], around[d]
        )

    for i in range(CHUNKS):
        receive(i)
        arrived(0, i)
        contract(0, [0], [0], i * span, span)
    for i in range(CHUNKS):
        receive(CHUNKS + i)
        for r in (1, ring - 1):
            arrived(r, i)
        contract(0, [1, ring - 1], [1, ring - 1], i * span, span)
        block, part = i // 2, i % 2
        if part == 0:
            block_in((ring - 1, 1)[block])
        lax.fori_loop(part * (mine // 2), (part + 1) * (mine // 2), transform, 0, unroll=8)
        if part == 1:
            image_done(1 + block)

    for c in range(CHUNKS):
        arrived(2, c)
        arrived(ring - 2, c)
    contract(0, [2, ring - 2], [2, ring - 2], 0, width)
    contract(1, [2], [3], 0, width)
    contract(2, [ring - 2], [ring - 3], 0, width)
    block_in(ring - 2)
    lax.fori_loop(0, mine, transform, 0, unroll=8)
    image_done(3)
    contract(3, [2], [4], 0, width)

    rows = ring * both
    part_x[x] = jnp.concatenate(
        [acc[pl.ds(n * width, width), :].T[:mine] for n in range(rows // width)], 1
    )
    for d in range(1, nx):
        send_x(d).start()
    receive(2 * CHUNKS)
    receive(2 * CHUNKS + 1)
    for d in range(1, nx):
        wait_x(d).wait_recv()
    total = part_x[0]
    for n in range(1, nx):
        total += part_x[n]
    part_z[z] = total
    for d in range(1, nz):
        send_z(d).start()
    receive(2 * CHUNKS + 2)
    for d in range(1, nz):
        wait_z(d).wait_recv()
    total = part_z[0]
    for n in range(1, nz):
        total += part_z[n]
    nblocks = fk.shape[0]
    row_parts[0][...] = (total * (2.0 / (nblocks * width))).astype(jnp.bfloat16)
    for d in range(1, ring):
        send_rows(d).start()
    receive(2 * CHUNKS + 3)
    for d in range(1, ring):
        send_rows(ring - d).wait_recv()

    place = lax.div(lax.broadcasted_iota(jnp.int32, (mine, rows), 1), both)

    def rows_of(d):
        near, after, before, far = [
            row_parts[(d + n) % ring][...].astype(jnp.float32) for n in (0, 1, ring - 1, 2)
        ]
        return jnp.where(
            place == 3, after, jnp.where(place == ring - 3, before, jnp.where(place == 4, far, near))
        )

    here, there = rows_of(0), rows_of(half)
    cut = half * both
    there = jnp.concatenate([there[:, cut:], there[:, :cut]], 1)
    low = jnp.zeros(here.shape, jnp.int32) + side == 0
    inter = jnp.concatenate(
        [jnp.where(low, here, there), jnp.where(low, there, here)], 0
    ).astype(jnp.bfloat16)
    factor = 1.0 / math.sqrt(rows)
    pair = 2

    def residual(i, carry):
        a = i * pair
        right = jnp.concatenate(
            [tiles[:, :, a + u].reshape(rows, width) for u in range(pair)], 1
        )
        made = dot(inter, right, NN) * factor
        for u in range(pair):
            zs[pl.ds((a + u) * both, both), :] = made[:, u * width : (u + 1) * width]
        return carry

    for i in range(middle):
        receive((half - 1) * CHUNKS + i)
        for c in (up_order[i], down_order[i]):
            for r in range(3, ring - 2):
                arrived(r, c)
            lax.fori_loop(c * span // pair, (c + 1) * span // pair, residual, 0, unroll=8)

    triangle = is_low * above_diag + side * below_diag
    keep = (off * is_low + (1 - off) * triangle) > 0

    def unpack(p, carry):
        tile = zs[pl.ds(p, width, stride=both), :]
        out[0, p] = jnp.where(keep, tile, -tile.T).astype(jnp.bfloat16)
        return carry

    lax.fori_loop(0, both, unpack, 0, unroll=4)

    for c in range(CHUNKS):
        exchange(c).wait_send()
        for r in range(ring):
            across(r, c).wait_send()
    for d in range(1, nx):
        send_x(d).wait_send()
    for d in range(1, nz):
        send_z(d).wait_send()
    for d in range(1, ring):
        send_rows(d).wait_send()


def body(sizes, amplitudes, fock_blocks, owner_map, extents):
    ring, nz, nx = sizes
    slots, both, width = amplitudes.shape[0], amplitudes.shape[1], amplitudes.shape[2]
    mine = both // 2
    half = ring // 2
    rows = ring * both
    dma = pltpu.SemaphoreType.DMA
    hbm = pl.BlockSpec(memory_space=pltpu.HBM)
    bf16, f32 = jnp.bfloat16, jnp.float32
    return pl.pallas_call(
        functools.partial(kernel, sizes),
        out_shape=jax.ShapeDtypeStruct((slots, both, width, width), bf16),
        in_specs=[hbm, hbm, hbm, hbm],
        out_specs=pl.BlockSpec(memory_space=pltpu.VMEM),
        scratch_shapes=[
            pltpu.SMEM(owner_map.shape[::-1], jnp.int32),
            pltpu.SMEM(extents.shape, jnp.int32),
            pltpu.VMEM((mine, width, width), bf16),
            pltpu.VMEM((mine, width, width), bf16),
            pltpu.VMEM(fock_blocks.shape, bf16),
            pltpu.VMEM((width * mine, width), f32),
            pltpu.VMEM((width * mine, width), f32),
            pltpu.VMEM((4, width, mine, width), bf16),
            pltpu.VMEM((ring, 2, width, mine, width), bf16),
            pltpu.VMEM((rows, width), f32),
            pltpu.VMEM((nx, mine, rows), f32),
            pltpu.VMEM((nz, mine, rows), f32),
            [pltpu.VMEM((mine, rows), bf16)] * ring,
            pltpu.VMEM((width * both, width), f32),
            dma((4,)),
            dma((CHUNKS,)), dma((CHUNKS,)),
            dma((half, CHUNKS)), dma((half, CHUNKS)),
            dma((half, CHUNKS)), dma((half, CHUNKS)),
            dma((ring, CHUNKS)), dma((ring, CHUNKS)),
            dma((nx,)), dma((nx,)),
            dma((nz,)), dma((nz,)),
            dma((ring,)), dma((ring,)),
        ],
        compiler_params=pltpu.CompilerParams(
            collective_id=0, has_side_effects=True, vmem_limit_bytes=63 * 1024 * 1024
        ),
        cost_estimate=pl.CostEstimate(
            flops=2**30, bytes_accessed=2**22, transcendentals=0
        ),
    )(amplitudes, fock_blocks, owner_map.T, extents)


def solution(mesh):
    plane = mesh.shape["vpair"] // 2
    nx = 4 if plane % 4 == 0 else 1
    sizes = (mesh.shape["occ"], plane // nx, nx)
    placed = (P("vpair", "occ", None, None), P(), P(), P())
    return jax.shard_map(
        functools.partial(body, sizes),
        mesh=mesh,
        in_specs=placed,
        out_specs=P("vpair", "occ", None, None),
        check_vma=False,
    )
```

```python
import functools
import math

import jax
import jax.numpy as jnp
from jax import lax
from jax.experimental import pallas as pl
from jax.experimental.pallas import tpu as pltpu
from jax.sharding import PartitionSpec as P

MESH = pl.DeviceIdType.MESH
CHUNKS = 4
DEPTH = 4
NT = (((1,), (1,)), ((), ()))
NN = (((1,), (0,)), ((), ()))


def dot(left, right, dims):
    return lax.dot_general(left, right, dims, preferred_element_type=jnp.float32)


def kernel(
    sizes,
    amps, fock, owner_at, extents_at, out,
    owner, extents, own, received, fk, xf, yf, hf, yb, tiles, acc, part_x, part_z, row_parts, zs,
    load_sem, ex_send, ex_recv, up_send, up_recv, down_send, down_recv,
    core_send, core_recv, x_send, x_recv, z_send, z_recv, row_send, row_recv,
):
    ring, nz, nx = sizes
    half = ring // 2
    per_side = ring // 2
    plane = nz * nx
    mine, width = own.shape[0], own.shape[1]
    both = 2 * mine
    group = mine // CHUNKS
    span = width // CHUNKS

    v = lax.axis_index("vpair")
    o = lax.axis_index("occ")
    side = lax.div(v, plane)
    w = lax.rem(v, plane)
    z = lax.div(w, nx)
    x = lax.rem(w, nx)
    core = lax.rem(o, 2)
    y = side * per_side + lax.div(o, 2)

    def device(y_at, core_at, w_at):
        return (
            lax.div(y_at, per_side) * plane + w_at,
            lax.rem(y_at, per_side) * 2 + core_at,
        )

    around = [device(lax.rem(y + d, ring), core, w) for d in range(ring)]
    mirror, above, below = around[half], around[1], around[ring - 1]
    sibling = device(y, 1 - core, w)
    x_at = [lax.rem(x + d, nx) for d in range(nx)]
    z_at = [lax.rem(z + d, nz) for d in range(nz)]
    x_peer = [device(y, core, z * nx + at) for at in x_at]
    z_peer = [device(y, core, at * nx + x) for at in z_at]

    loads = [
        pltpu.make_async_copy(
            amps.at[0, pl.ds(side * mine, mine)], own, load_sem.at[0]
        ),
        pltpu.make_async_copy(fock, fk, load_sem.at[1]),
        pltpu.make_async_copy(owner_at, owner, load_sem.at[2]),
        pltpu.make_async_copy(extents_at, extents, load_sem.at[3]),
    ]
    for copy in loads:
        copy.start()

    peers = around[1:] + [sibling] + x_peer[1:] + z_peer[1:]
    barrier = pltpu.get_barrier_semaphore()
    for peer in peers:
        pl.semaphore_signal(barrier, inc=1, device_id=peer, device_id_type=MESH)
    pl.semaphore_wait(barrier, len(peers))

    def remote(src, dst, send, recv, to):
        return pltpu.make_async_remote_copy(
            src_ref=src, dst_ref=dst, send_sem=send, recv_sem=recv,
            device_id=to, device_id_type=MESH,
        )

    def exchange(c):
        return remote(
            amps.at[0, pl.ds((1 - side) * mine + c * group, group)],
            received.at[pl.ds(c * group, group)],
            ex_send.at[c], ex_recv.at[c], mirror,
        )

    for c in range(CHUNKS):
        exchange(c).start()

    for copy in loads:
        copy.wait()

    lower_slot = w
    upper_slot = w + plane
    a_low, b_low = owner[0, lower_slot], owner[1, lower_slot]
    a_high, b_high = owner[0, upper_slot], owner[1, upper_slot]
    off = (a_low != b_low).astype(jnp.int32)
    is_low = 1 - side
    row = lax.broadcasted_iota(jnp.int32, (width, width), 0)
    col = lax.broadcasted_iota(jnp.int32, (width, width), 1)
    above_diag = jnp.where(row < col, 1, 0)
    below_diag = jnp.where(row > col, 1, 0)
    first_i = jnp.minimum(above_diag + off, 1)
    second_i = below_diag * (1 - off)
    first = first_i > 0
    live = (row < jnp.where(first, extents[a_low], extents[a_high])) & (
        col < jnp.where(first, extents[b_low], extents[b_high])
    )
    plus_own = first_i == is_low
    minus_own = second_i == is_low

    fock_a1, fock_b1 = fk[a_low], fk[b_low]
    fock_a2, fock_b2 = fk[a_high], fk[b_high]

    acc[...] = jnp.zeros_like(acc)

    def build(p, carry):
        mine_t = own[p].astype(jnp.float32)
        other_t = received[p].astype(jnp.float32)
        plus = jnp.where(plus_own, mine_t, other_t)
        minus = jnp.where(minus_own, mine_t, other_t)
        xf[pl.ds(p, width, stride=mine), :] = jnp.where(live, plus - minus.T, 0.0)
        return carry

    for c in range(CHUNKS):
        exchange(c).wait_recv()
        lax.fori_loop(c * group, (c + 1) * group, build, 0, unroll=4)

    def up(t, c):
        at = lax.rem(ring - t, ring) if not isinstance(t, int) else (ring - t) % ring
        return remote(
            tiles.at[at, 0, pl.ds(c * span, span)],
            tiles.at[ring - 1 - t, 0, pl.ds(c * span, span)],
            up_send.at[t, c], up_recv.at[t, c], above,
        )

    def down(t, c):
        return remote(
            tiles.at[t, 0, pl.ds(c * span, span)],
            tiles.at[t + 1, 0, pl.ds(c * span, span)],
            down_send.at[t, c], down_recv.at[t, c], below,
        )

    def across(r, c):
        return remote(
            tiles.at[r, 0, pl.ds(c * span, span)],
            tiles.at[r, 1, pl.ds(c * span, span)],
            core_send.at[r, c], core_recv.at[r, c], sibling,
        )

    middle = CHUNKS // 2
    up_order = list(range(CHUNKS))
    down_order = up_order[middle:] + up_order[:middle]
    up_steps = [(t, c) for t in range(half) for c in up_order][: -middle]
    down_steps = [(t, c) for t in range(half) for c in down_order][: -middle]

    def start(i):
        if i < len(up_steps):
            up(*up_steps[i]).start()
            down(*down_steps[i]).start()

    def own_chunk(c):
        block = xf[pl.ds(c * span * mine, span * mine), :].astype(jnp.bfloat16)
        tiles[0, 0, pl.ds(c * span, span)] = block.reshape(span, mine, width)

    for i in range(CHUNKS):
        if i < middle:
            own_chunk(up_order[i])
            own_chunk(down_order[i])
        if i < DEPTH:
            start(i)
    for c in range(CHUNKS):
        across(0, c).start()

    def right_factor(n, r, c):
        block = tiles[r, 0, pl.ds(c * span, span)].reshape(span * mine, width)
        block = block.astype(jnp.float32)
        at_a = lax.div(lax.broadcasted_iota(jnp.int32, block.shape, 0), mine) + c * span
        at_b = lax.broadcasted_iota(jnp.int32, block.shape, 1)
        upper = jnp.where(at_a < at_b, 1, 0) + off > 0
        for m, (keep_here, factor_b) in enumerate(((upper, fock_b1), (at_a > at_b, fock_b2))):
            part = jnp.where(keep_here, block, 0.0).astype(jnp.bfloat16)
            made = dot(part, factor_b, NT).astype(jnp.bfloat16)
            hf[n, m, pl.ds(c * span * mine, span * mine), :] = made.astype(jnp.float32)

    def left_factor(n, to):
        def some(p, carry):
            one = hf[n, 0, pl.ds(p, width, stride=mine), :].astype(jnp.bfloat16)
            two = hf[n, 1, pl.ds(p, width, stride=mine), :].astype(jnp.bfloat16)
            one, two = dot(fock_a1, one, NN), dot(fock_a2, two, NN)
            turned = jnp.where(below_diag > 0, one, two).T
            yf[pl.ds(p, width, stride=mine), :] = jnp.where(first, one, two) - jnp.where(
                off > 0, 0.0, turned
            )
            return carry

        def narrow(c, carry):
            block = yf[pl.ds(c * span * mine, span * mine), :].astype(jnp.bfloat16)
            yb[to, pl.ds(c * span, span)] = block.reshape(span, mine, width)
            return carry

        lax.fori_loop(0, mine, some, 0, unroll=mine)
        lax.fori_loop(0, CHUNKS, narrow, 0)

    unroll = min(32, span)

    def contract(images, slots, to, begin, count):
        def some(i, sums):
            lefts, rights = [], []
            for u in range(unroll):
                a = begin + i * unroll + u
                rights.append(jnp.concatenate([yb[n, a] for n in images], 0))
                lefts.append(
                    jnp.concatenate([tiles[r, k, a] for r in slots for k in (0, 1)], 0)
                )
            return sums + dot(
                jnp.concatenate(lefts, 1), jnp.concatenate(rights, 1), NT
            )

        zero = jnp.zeros((len(slots) * both, len(images) * mine), jnp.float32)
        sums = lax.fori_loop(0, count // unroll, some, zero, unroll=count // unroll)
        for m in range(len(slots)):
            for n in range(len(images)):
                made = sums[m * both : (m + 1) * both, n * mine : (n + 1) * mine]
                acc[pl.ds(to[m][n] * both, both), pl.ds(0, mine)] += made

    def receive(i):
        t, c = up_steps[i]
        up(t, c).wait_recv()
        up(t, c).wait_send()
        across(ring - 1 - t, c).start()
        t, c = down_steps[i]
        down(t, c).wait_recv()
        down(t, c).wait_send()
        across(t + 1, c).start()
        start(i + DEPTH)

    def arrived(r, c):
        across(r, c).wait_recv()

    def send_x(d):
        return remote(part_x.at[x], part_x.at[x], x_send.at[d], x_recv.at[x], x_peer[d])

    def wait_x(d):
        return remote(
            part_x.at[x_at[d]], part_x.at[x_at[d]], x_send.at[d], x_recv.at[x_at[d]], x_peer[d]
        )

    def send_z(d):
        return remote(part_z.at[z], part_z.at[z], z_send.at[d], z_recv.at[z], z_peer[d])

    def wait_z(d):
        return remote(
            part_z.at[z_at[d]], part_z.at[z_at[d]], z_send.at[d], z_recv.at[z_at[d]], z_peer[d]
        )

    def send_rows(d):
        return remote(
            row_parts[0], row_parts[ring - d], row_send.at[d], row_recv.at[ring - d], around[d]
        )

    last = ring - 1
    for c in range(CHUNKS):
        right_factor(0, 0, c)
    left_factor(0, 0)
    for i in range(CHUNKS):
        receive(i)
        right_factor(0, last, up_order[i])
        right_factor(1, 1, down_order[i])
        arrived(0, i)
        if i == middle:
            contract([0], [0], [[0]], 0, width // 2)
    contract([0], [0], [[0]], width // 2, width // 2)

    halves = (0, width // 2)
    for i in range(CHUNKS):
        receive(CHUNKS + i)
        right_factor(2, last - 1, up_order[i])
        if i == 0:
            for c in range(CHUNKS):
                arrived(1, c)
                arrived(last, c)
        if i < 2:
            left_factor(i, 1 + i)
        if i == 1:
            contract([0], [1, last], [[1], [last]], 0, width)
        if i == 2:
            for j in range(middle):
                arrived(2, down_order[j])
                arrived(last - 1, up_order[j])
            contract([0, 1], [2], [[2, 3]], halves[1], width // 2)
            contract([0, 2], [last - 1], [[last - 1, last - 2]], halves[0], width // 2)
    left_factor(2, 3)
    for j in range(middle, CHUNKS):
        arrived(2, down_order[j])
        arrived(last - 1, up_order[j])
    contract([0, 1], [2], [[2, 3]], halves[0], width // 2)
    contract([0, 2], [last - 1], [[last - 1, last - 2]], halves[1], width // 2)
    contract([3], [2], [[4]], 0, width)

    rows = ring * both
    part_x[x] = jnp.concatenate(
        [acc[pl.ds(n * width, width), :].T[:mine] for n in range(rows // width)], 1
    )
    for d in range(1, nx):
        send_x(d).start()
    receive(2 * CHUNKS)
    receive(2 * CHUNKS + 1)
    for d in range(1, nx):
        wait_x(d).wait_recv()
    total = part_x[0]
    for n in range(1, nx):
        total += part_x[n]
    part_z[z] = total
    for d in range(1, nz):
        send_z(d).start()
    receive(2 * CHUNKS + 2)
    for d in range(1, nz):
        wait_z(d).wait_recv()
    total = part_z[0]
    for n in range(1, nz):
        total += part_z[n]
    nblocks = fk.shape[0]
    row_parts[0][...] = (total * (2.0 / (nblocks * width))).astype(jnp.bfloat16)
    for d in range(1, ring):
        send_rows(d).start()
    receive(2 * CHUNKS + 3)
    for d in range(1, ring):
        send_rows(ring - d).wait_recv()

    place = lax.div(lax.broadcasted_iota(jnp.int32, (mine, rows), 1), both)

    def rows_of(d):
        near, after, before, far = [
            row_parts[(d + n) % ring][...].astype(jnp.float32) for n in (0, 1, ring - 1, 2)
        ]
        return jnp.where(
            place == 3, after, jnp.where(place == ring - 3, before, jnp.where(place == 4, far, near))
        )

    here, there = rows_of(0), rows_of(half)
    cut = half * both
    there = jnp.concatenate([there[:, cut:], there[:, :cut]], 1)
    low = jnp.zeros(here.shape, jnp.int32) + side == 0
    inter = jnp.concatenate(
        [jnp.where(low, here, there), jnp.where(low, there, here)], 0
    ).astype(jnp.bfloat16)
    factor = 1.0 / math.sqrt(rows)
    pair = 2

    def residual(i, carry):
        a = i * pair
        right = jnp.concatenate(
            [tiles[:, :, a + u].reshape(rows, width) for u in range(pair)], 1
        )
        made = dot(inter, right, NN) * factor
        for u in range(pair):
            zs[pl.ds((a + u) * both, both), :] = made[:, u * width : (u + 1) * width]
        return carry

    for i in range(middle):
        receive((half - 1) * CHUNKS + i)
        for c in (up_order[i], down_order[i]):
            for r in range(3, ring - 2):
                arrived(r, c)
            lax.fori_loop(c * span // pair, (c + 1) * span // pair, residual, 0, unroll=16)

    triangle = is_low * above_diag + side * below_diag
    keep = (off * is_low + (1 - off) * triangle) > 0

    def unpack(p, carry):
        tile = zs[pl.ds(p, width, stride=both), :]
        out[0, p] = jnp.where(keep, tile, -tile.T).astype(jnp.bfloat16)
        return carry

    lax.fori_loop(0, both, unpack, 0, unroll=8)

    for c in range(CHUNKS):
        exchange(c).wait_send()
        for r in range(ring):
            across(r, c).wait_send()
    for d in range(1, nx):
        send_x(d).wait_send()
    for d in range(1, nz):
        send_z(d).wait_send()
    for d in range(1, ring):
        send_rows(d).wait_send()


def body(sizes, amplitudes, fock_blocks, owner_map, extents):
    ring, nz, nx = sizes
    slots, both, width = amplitudes.shape[0], amplitudes.shape[1], amplitudes.shape[2]
    mine = both // 2
    half = ring // 2
    rows = ring * both
    dma = pltpu.SemaphoreType.DMA
    hbm = pl.BlockSpec(memory_space=pltpu.HBM)
    bf16, f32 = jnp.bfloat16, jnp.float32
    return pl.pallas_call(
        functools.partial(kernel, sizes),
        out_shape=jax.ShapeDtypeStruct((slots, both, width, width), bf16),
        in_specs=[hbm, hbm, hbm, hbm],
        out_specs=pl.BlockSpec(memory_space=pltpu.VMEM),
        scratch_shapes=[
            pltpu.SMEM(owner_map.shape[::-1], jnp.int32),
            pltpu.SMEM(extents.shape, jnp.int32),
            pltpu.VMEM((mine, width, width), bf16),
            pltpu.VMEM((mine, width, width), bf16),
            pltpu.VMEM(fock_blocks.shape, bf16),
            pltpu.VMEM((width * mine, width), f32),
            pltpu.VMEM((width * mine, width), f32),
            pltpu.VMEM((3, 2, width * mine, width), f32),
            pltpu.VMEM((4, width, mine, width), bf16),
            pltpu.VMEM((ring, 2, width, mine, width), bf16),
            pltpu.VMEM((rows, width), f32),
            pltpu.VMEM((nx, mine, rows), f32),
            pltpu.VMEM((nz, mine, rows), f32),
            [pltpu.VMEM((mine, rows), bf16)] * ring,
            pltpu.VMEM((width * both, width), f32),
            dma((4,)),
            dma((CHUNKS,)), dma((CHUNKS,)),
            dma((half, CHUNKS)), dma((half, CHUNKS)),
            dma((half, CHUNKS)), dma((half, CHUNKS)),
            dma((ring, CHUNKS)), dma((ring, CHUNKS)),
            dma((nx,)), dma((nx,)),
            dma((nz,)), dma((nz,)),
            dma((ring,)), dma((ring,)),
        ],
        compiler_params=pltpu.CompilerParams(
            collective_id=0, has_side_effects=True, vmem_limit_bytes=48 * 1024 * 1024
        ),
        cost_estimate=pl.CostEstimate(
            flops=2**30, bytes_accessed=2**22, transcendentals=0
        ),
    )(*[
        pltpu.with_memory_space_constraint(value, pltpu.HBM)
        for value in (amplitudes, fock_blocks, owner_map.T, extents)
    ])


def solution(mesh):
    plane = mesh.shape["vpair"] // 2
    nx = 4 if plane % 4 == 0 else 1
    sizes = (mesh.shape["occ"], plane // nx, nx)
    placed = (P("vpair", "occ", None, None), P(), P(), P())
    return jax.shard_map(
        functools.partial(body, sizes),
        mesh=mesh,
        in_specs=placed,
        out_specs=P("vpair", "occ", None, None),
        check_vma=False,
    )
```

```python
import functools
import math

import jax
import jax.numpy as jnp
from jax import lax
from jax.experimental import pallas as pl
from jax.experimental.pallas import tpu as pltpu
from jax.sharding import PartitionSpec as P

MESH = pl.DeviceIdType.MESH
CHUNKS = 4
NT = (((1,), (1,)), ((), ()))
NN = (((1,), (0,)), ((), ()))


def dot(left, right, dims):
    return lax.dot_general(left, right, dims, preferred_element_type=jnp.float32)


def kernel(
    sizes,
    amps, fock, owner_at, extents_at, out,
    owner, extents, from_below, from_above, fk, xf, yf, hf, yb, tiles, acc, part_x, part_z, row_left, row_right, zs,
    load_sem, ex_up_send, ex_up_recv, ex_down_send, ex_down_recv, up_send, up_recv, down_send, down_recv,
    core_send, core_recv, x_send, x_recv, z_send, z_recv, left_send, left_recv, right_send, right_recv,
):
    ring, nz, nx = sizes
    half = ring // 2
    per_side = ring // 2
    plane = nz * nx
    mine, width = from_below.shape[0], from_below.shape[1]
    both = 2 * mine
    group = mine // CHUNKS
    span = width // CHUNKS

    v = lax.axis_index("vpair")
    o = lax.axis_index("occ")
    side = lax.div(v, plane)
    w = lax.rem(v, plane)
    z = lax.div(w, nx)
    x = lax.rem(w, nx)
    core = lax.rem(o, 2)
    y = side * per_side + lax.div(o, 2)

    def device(y_at, core_at, w_at):
        return (
            lax.div(y_at, per_side) * plane + w_at,
            lax.rem(y_at, per_side) * 2 + core_at,
        )

    around = [device(lax.rem(y + d, ring), core, w) for d in range(ring)]
    above, below = around[1], around[ring - 1]
    sibling = device(y, 1 - core, w)
    x_at = [lax.rem(x + d, nx) for d in range(nx)]
    z_at = [lax.rem(z + d, nz) for d in range(nz)]
    x_peer = [device(y, core, z * nx + at) for at in x_at]
    z_peer = [device(y, core, at * nx + x) for at in z_at]

    loads = [
        pltpu.make_async_copy(fock, fk, load_sem.at[1]),
        pltpu.make_async_copy(owner_at, owner, load_sem.at[2]),
        pltpu.make_async_copy(extents_at, extents, load_sem.at[0]),
    ]
    for copy in loads:
        copy.start()

    peers = around[1:] + [sibling] + x_peer[1:] + z_peer[1:]
    barrier = pltpu.get_barrier_semaphore()
    for peer in peers:
        pl.semaphore_signal(barrier, inc=1, device_id=peer, device_id_type=MESH)
    pl.semaphore_wait(barrier, len(peers))

    def remote(src, dst, send, recv, to):
        return pltpu.make_async_remote_copy(
            src_ref=src, dst_ref=dst, send_sem=send, recv_sem=recv,
            device_id=to, device_id_type=MESH,
        )

    reach = half // 2

    def exchange_up(c):
        return remote(
            amps.at[0, pl.ds(side * mine + c * group, group)],
            from_below.at[pl.ds(c * group, group)],
            ex_up_send.at[c], ex_up_recv.at[c], around[reach],
        )

    def exchange_down(c):
        return remote(
            amps.at[0, pl.ds((1 - side) * mine + c * group, group)],
            from_above.at[pl.ds(c * group, group)],
            ex_down_send.at[c], ex_down_recv.at[c], around[ring - reach],
        )

    for c in range(CHUNKS):
        exchange_up(c).start()
        exchange_down(c).start()

    for copy in loads:
        copy.wait()

    lower_slot = w
    upper_slot = w + plane
    a_low, b_low = owner[0, lower_slot], owner[1, lower_slot]
    a_high, b_high = owner[0, upper_slot], owner[1, upper_slot]
    off = (a_low != b_low).astype(jnp.int32)
    is_low = 1 - side
    below_is_low = lax.div(lax.rem(y + ring - reach, ring), half) == 0
    below_is_low = below_is_low.astype(jnp.int32)
    row = lax.broadcasted_iota(jnp.int32, (width, width), 0)
    col = lax.broadcasted_iota(jnp.int32, (width, width), 1)
    above_diag = jnp.where(row < col, 1, 0)
    below_diag = jnp.where(row > col, 1, 0)
    first_i = jnp.minimum(above_diag + off, 1)
    second_i = below_diag * (1 - off)
    first = first_i > 0
    live = (row < jnp.where(first, extents[a_low], extents[a_high])) & (
        col < jnp.where(first, extents[b_low], extents[b_high])
    )
    plus_below = first_i == below_is_low
    minus_below = second_i == below_is_low

    fock_a1, fock_b1 = fk[a_low], fk[b_low]
    fock_a2, fock_b2 = fk[a_high], fk[b_high]

    acc[...] = jnp.zeros_like(acc)

    def build(p, carry):
        one = from_below[p].astype(jnp.float32)
        two = from_above[p].astype(jnp.float32)
        plus = jnp.where(plus_below, one, two)
        minus = jnp.where(minus_below, one, two)
        xf[pl.ds(p, width, stride=mine), :] = jnp.where(live, plus - minus.T, 0.0)
        return carry

    for c in range(CHUNKS):
        exchange_up(c).wait_recv()
        exchange_down(c).wait_recv()
        lax.fori_loop(c * group, (c + 1) * group, build, 0, unroll=4)

    def up(t, c):
        at = lax.rem(ring - t, ring) if not isinstance(t, int) else (ring - t) % ring
        return remote(
            tiles.at[at, 0, pl.ds(c * span, span)],
            tiles.at[ring - 1 - t, 0, pl.ds(c * span, span)],
            up_send.at[t, c], up_recv.at[t, c], above,
        )

    def down(t, c):
        return remote(
            tiles.at[t, 0, pl.ds(c * span, span)],
            tiles.at[t + 1, 0, pl.ds(c * span, span)],
            down_send.at[t, c], down_recv.at[t, c], below,
        )

    def across(r, c):
        return remote(
            tiles.at[r, 0, pl.ds(c * span, span)],
            tiles.at[r, 1, pl.ds(c * span, span)],
            core_send.at[r, c], core_recv.at[r, c], sibling,
        )

    middle = CHUNKS // 2
    up_order = list(range(CHUNKS))
    down_order = up_order[middle:] + up_order[:middle]
    up_steps = [(t, c) for t in range(half) for c in up_order][: -middle]
    down_steps = [(t, c) for t in range(half) for c in down_order][: -middle]

    def own_chunk(c):
        block = xf[pl.ds(c * span * mine, span * mine), :].astype(jnp.bfloat16)
        tiles[0, 0, pl.ds(c * span, span)] = block.reshape(span, mine, width)

    for i in range(CHUNKS):
        if i < middle:
            own_chunk(up_order[i])
            own_chunk(down_order[i])
        up(*up_steps[i]).start()
        down(*down_steps[i]).start()
    for c in range(CHUNKS):
        across(0, c).start()

    def right_factor(n, r, c):
        block = tiles[r, 0, pl.ds(c * span, span)].reshape(span * mine, width)
        block = block.astype(jnp.float32)
        at_a = lax.div(lax.broadcasted_iota(jnp.int32, block.shape, 0), mine) + c * span
        at_b = lax.broadcasted_iota(jnp.int32, block.shape, 1)
        upper = jnp.where(at_a < at_b, 1, 0) + off > 0
        for m, (keep_here, factor_b) in enumerate(((upper, fock_b1), (at_a > at_b, fock_b2))):
            part = jnp.where(keep_here, block, 0.0).astype(jnp.bfloat16)
            made = dot(part, factor_b, NT).astype(jnp.bfloat16)
            hf[n, m, pl.ds(c * span * mine, span * mine), :] = made.astype(jnp.float32)

    def left_factor(n, to):
        def some(p, carry):
            one = hf[n, 0, pl.ds(p, width, stride=mine), :].astype(jnp.bfloat16)
            two = hf[n, 1, pl.ds(p, width, stride=mine), :].astype(jnp.bfloat16)
            one, two = dot(fock_a1, one, NN), dot(fock_a2, two, NN)
            turned = jnp.where(below_diag > 0, one, two).T
            yf[pl.ds(p, width, stride=mine), :] = jnp.where(first, one, two) - jnp.where(
                off > 0, 0.0, turned
            )
            return carry

        def narrow(c, carry):
            block = yf[pl.ds(c * span * mine, span * mine), :].astype(jnp.bfloat16)
            yb[to, pl.ds(c * span, span)] = block.reshape(span, mine, width)
            return carry

        lax.fori_loop(0, mine, some, 0, unroll=mine)
        lax.fori_loop(0, CHUNKS, narrow, 0)

    unroll = min(32, span)

    def contract(images, slots, to, begin, count):
        def some(i, sums):
            lefts, rights = [], []
            for u in range(unroll):
                a = begin + i * unroll + u
                rights.append(jnp.concatenate([yb[n, a] for n in images], 0))
                lefts.append(
                    jnp.concatenate([tiles[r, k, a] for r in slots for k in (0, 1)], 0)
                )
            return sums + dot(
                jnp.concatenate(lefts, 1), jnp.concatenate(rights, 1), NT
            )

        zero = jnp.zeros((len(slots) * both, len(images) * mine), jnp.float32)
        sums = lax.fori_loop(0, count // unroll, some, zero, unroll=count // unroll)
        for m in range(len(slots)):
            for n in range(len(images)):
                made = sums[m * both : (m + 1) * both, n * mine : (n + 1) * mine]
                acc[pl.ds(to[m][n] * both, both), pl.ds(0, mine)] += made

    def receive(i):
        t, c = up_steps[i]
        up(t, c).wait_recv()
        if i + CHUNKS < len(up_steps):
            up(*up_steps[i + CHUNKS]).start()
        across(ring - 1 - t, c).start()
        t, c = down_steps[i]
        down(t, c).wait_recv()
        if i + CHUNKS < len(down_steps):
            down(*down_steps[i + CHUNKS]).start()
        across(t + 1, c).start()

    def arrived(r, c):
        across(r, c).wait_recv()

    def send_x(d):
        return remote(part_x.at[x], part_x.at[x], x_send.at[d], x_recv.at[x], x_peer[d])

    def wait_x(d):
        return remote(
            part_x.at[x_at[d]], part_x.at[x_at[d]], x_send.at[d], x_recv.at[x_at[d]], x_peer[d]
        )

    def send_z(d):
        return remote(part_z.at[z], part_z.at[z], z_send.at[d], z_recv.at[z], z_peer[d])

    def wait_z(d):
        return remote(
            part_z.at[z_at[d]], part_z.at[z_at[d]], z_send.at[d], z_recv.at[z_at[d]], z_peer[d]
        )

    left_to = (1, 2, ring - 3, ring - 2)
    right_to = (2, 3, half, ring - 2, ring - 1)

    def send_left(d):
        return remote(
            row_left[0], row_left[ring - d], left_send.at[d], left_recv.at[ring - d], around[d]
        )

    def send_right(d):
        return remote(
            row_right[0], row_right[ring - d], right_send.at[d], right_recv.at[ring - d], around[d]
        )

    def row_sends():
        return [send_left(d) for d in left_to] + [send_right(d) for d in right_to]

    last = ring - 1
    for c in range(CHUNKS):
        right_factor(0, 0, c)
    left_factor(0, 0)
    for i in range(CHUNKS):
        receive(i)
        right_factor(0, last, up_order[i])
        right_factor(1, 1, down_order[i])
        arrived(0, i)
        if i == middle:
            contract([0], [0], [[0]], 0, width // 2)
    contract([0], [0], [[0]], width // 2, width // 2)

    halves = (0, width // 2)
    for i in range(CHUNKS):
        receive(CHUNKS + i)
        right_factor(2, last - 1, up_order[i])
        if i == 0:
            for c in range(CHUNKS):
                arrived(1, c)
                arrived(last, c)
        if i < 2:
            left_factor(i, 1 + i)
        if i == 1:
            contract([0], [1, last], [[1], [last]], 0, width)
        if i == 2:
            for j in range(middle):
                arrived(2, down_order[j])
                arrived(last - 1, up_order[j])
            contract([0, 1], [2], [[2, 3]], halves[1], width // 2)
            contract([0, 2], [last - 1], [[last - 1, last - 2]], halves[0], width // 2)
    left_factor(2, 3)
    for j in range(middle, CHUNKS):
        arrived(2, down_order[j])
        arrived(last - 1, up_order[j])
    contract([0, 1], [2], [[2, 3]], halves[0], width // 2)
    contract([0, 2], [last - 1], [[last - 1, last - 2]], halves[1], width // 2)
    contract([3], [2], [[4]], 0, width)

    rows = ring * both
    part_x[x] = jnp.concatenate(
        [acc[pl.ds(n * width, width), :].T[:mine] for n in range(rows // width)], 1
    )
    for d in range(1, nx):
        send_x(d).start()
    receive(2 * CHUNKS)
    receive(2 * CHUNKS + 1)
    for d in range(1, nx):
        wait_x(d).wait_recv()
    total = part_x[0]
    for n in range(1, nx):
        total += part_x[n]
    part_z[z] = total
    for d in range(1, nz):
        send_z(d).start()
    receive(2 * CHUNKS + 2)
    for d in range(1, nz):
        wait_z(d).wait_recv()
    total = part_z[0]
    for n in range(1, nz):
        total += part_z[n]
    nblocks = fk.shape[0]
    made = (total * (2.0 / (nblocks * width))).astype(jnp.bfloat16)
    row_left[0][...] = made[:, : rows // 2]
    row_right[0][...] = made[:, rows // 2 :]
    for copy in row_sends():
        copy.start()
    receive(2 * CHUNKS + 3)
    receive(3 * CHUNKS)
    receive(3 * CHUNKS + 1)
    for copy in row_sends():
        copy.wait_recv()

    place = lax.div(lax.broadcasted_iota(jnp.int32, (mine, rows // 2), 1), both)

    def rows_of(d):
        left = jnp.where(
            place == 3,
            row_left[(d + 1) % ring][...].astype(jnp.float32),
            row_left[d][...].astype(jnp.float32),
        )
        right = jnp.where(
            place == 0,
            row_right[(d + 2) % ring][...].astype(jnp.float32),
            jnp.where(
                place == 1,
                row_right[d - 1][...].astype(jnp.float32),
                row_right[d][...].astype(jnp.float32),
            ),
        )
        return pltpu.roll(jnp.concatenate([left, right], 1), d * both, 1)

    here, there = rows_of(reach), rows_of(ring - reach)
    low = jnp.zeros(here.shape, jnp.int32) + side == 0
    inter = jnp.concatenate(
        [jnp.where(low, here, there), jnp.where(low, there, here)], 0
    ).astype(jnp.bfloat16)
    factor = 1.0 / math.sqrt(rows)
    pair = 2

    def residual(i, carry):
        a = i * pair
        right = jnp.concatenate(
            [tiles[:, :, a + u].reshape(rows, width) for u in range(pair)], 1
        )
        made = dot(inter, right, NN) * factor
        for u in range(pair):
            zs[pl.ds((a + u) * both, both), :] = made[:, u * width : (u + 1) * width]
        return carry

    for i in range(middle):
        for c in (up_order[i], down_order[i]):
            for r in range(3, ring - 2):
                arrived(r, c)
            lax.fori_loop(c * span // pair, (c + 1) * span // pair, residual, 0, unroll=16)

    triangle = is_low * above_diag + side * below_diag
    keep = (off * is_low + (1 - off) * triangle) > 0

    def unpack(p, carry):
        tile = zs[pl.ds(p, width, stride=both), :]
        out[0, p] = jnp.where(keep, tile, -tile.T).astype(jnp.bfloat16)
        return carry

    lax.fori_loop(0, both, unpack, 0, unroll=8)

    for c in range(CHUNKS):
        exchange_up(c).wait_send()
        exchange_down(c).wait_send()
        for r in range(ring):
            across(r, c).wait_send()
    for i in range(len(up_steps)):
        up(*up_steps[i]).wait_send()
        down(*down_steps[i]).wait_send()
    for d in range(1, nx):
        send_x(d).wait_send()
    for d in range(1, nz):
        send_z(d).wait_send()
    for copy in row_sends():
        copy.wait_send()


def body(sizes, amplitudes, fock_blocks, owner_map, extents):
    ring, nz, nx = sizes
    slots, both, width = amplitudes.shape[0], amplitudes.shape[1], amplitudes.shape[2]
    mine = both // 2
    half = ring // 2
    rows = ring * both
    dma = pltpu.SemaphoreType.DMA
    hbm = pl.BlockSpec(memory_space=pltpu.HBM)
    bf16, f32 = jnp.bfloat16, jnp.float32
    return pl.pallas_call(
        functools.partial(kernel, sizes),
        out_shape=jax.ShapeDtypeStruct((slots, both, width, width), bf16),
        in_specs=[hbm, hbm, hbm, hbm],
        out_specs=pl.BlockSpec(memory_space=pltpu.VMEM),
        scratch_shapes=[
            pltpu.SMEM(owner_map.shape[::-1], jnp.int32),
            pltpu.SMEM(extents.shape, jnp.int32),
            pltpu.VMEM((mine, width, width), bf16),
            pltpu.VMEM((mine, width, width), bf16),
            pltpu.VMEM(fock_blocks.shape, bf16),
            pltpu.VMEM((width * mine, width), f32),
            pltpu.VMEM((width * mine, width), f32),
            pltpu.VMEM((3, 2, width * mine, width), f32),
            pltpu.VMEM((4, width, mine, width), bf16),
            pltpu.VMEM((ring, 2, width, mine, width), bf16),
            pltpu.VMEM((rows, width), f32),
            pltpu.VMEM((nx, mine, rows), f32),
            pltpu.VMEM((nz, mine, rows), f32),
            [pltpu.VMEM((mine, rows // 2), bf16)] * ring,
            [pltpu.VMEM((mine, rows // 2), bf16)] * ring,
            pltpu.VMEM((width * both, width), f32),
            dma((3,)),
            dma((CHUNKS,)), dma((CHUNKS,)), dma((CHUNKS,)), dma((CHUNKS,)),
            dma((half, CHUNKS)), dma((half, CHUNKS)),
            dma((half, CHUNKS)), dma((half, CHUNKS)),
            dma((ring, CHUNKS)), dma((ring, CHUNKS)),
            dma((nx,)), dma((nx,)),
            dma((nz,)), dma((nz,)),
            dma((ring,)), dma((ring,)), dma((ring,)), dma((ring,)),
        ],
        compiler_params=pltpu.CompilerParams(
            collective_id=0, has_side_effects=True, vmem_limit_bytes=48 * 1024 * 1024
        ),
        cost_estimate=pl.CostEstimate(
            flops=2**30, bytes_accessed=2**22, transcendentals=0
        ),
    )(*[
        pltpu.with_memory_space_constraint(value, pltpu.HBM)
        for value in (amplitudes, fock_blocks, owner_map.T, extents)
    ])


def solution(mesh):
    plane = mesh.shape["vpair"] // 2
    nx = 4 if plane % 4 == 0 else 1
    sizes = (mesh.shape["occ"], plane // nx, nx)
    placed = (P("vpair", "occ", None, None), P(), P(), P())
    return jax.shard_map(
        functools.partial(body, sizes),
        mesh=mesh,
        in_specs=placed,
        out_specs=P("vpair", "occ", None, None),
        check_vma=False,
    )
```

```python
import functools
import math

import jax
import jax.numpy as jnp
from jax import lax
from jax.experimental import pallas as pl
from jax.experimental.pallas import tpu as pltpu
from jax.sharding import PartitionSpec as P

MESH = pl.DeviceIdType.MESH
CHUNKS = 4
NT = (((1,), (1,)), ((), ()))
NN = (((1,), (0,)), ((), ()))


def dot(left, right, dims):
    return lax.dot_general(left, right, dims, preferred_element_type=jnp.float32)


def kernel(
    sizes,
    amps, fock, owner_at, extents_at, out,
    owner, extents, from_below, from_above, fk, xf, yf, hf, yb, tiles, acc, part_x, part_z, row_left, row_right, zs,
    load_sem, ex_up_send, ex_up_recv, ex_down_send, ex_down_recv, up_send, up_recv, down_send, down_recv,
    core_send, core_recv, x_send, x_recv, z_send, z_recv, left_send, left_recv, right_send, right_recv,
):
    ring, nz, nx = sizes
    half = ring // 2
    per_side = ring // 2
    plane = nz * nx
    mine, width = from_below.shape[0], from_below.shape[1]
    both = 2 * mine
    group = mine // CHUNKS
    span = width // CHUNKS

    v = lax.axis_index("vpair")
    o = lax.axis_index("occ")
    side = lax.div(v, plane)
    w = lax.rem(v, plane)
    z = lax.div(w, nx)
    x = lax.rem(w, nx)
    core = lax.rem(o, 2)
    y = side * per_side + lax.div(o, 2)

    def device(y_at, core_at, w_at):
        return (
            lax.div(y_at, per_side) * plane + w_at,
            lax.rem(y_at, per_side) * 2 + core_at,
        )

    around = [device(lax.rem(y + d, ring), core, w) for d in range(ring)]
    above, below = around[1], around[ring - 1]
    sibling = device(y, 1 - core, w)
    x_at = [lax.rem(x + d, nx) for d in range(nx)]
    z_at = [lax.rem(z + d, nz) for d in range(nz)]
    x_peer = [device(y, core, z * nx + at) for at in x_at]
    z_peer = [device(y, core, at * nx + x) for at in z_at]

    loads = [
        pltpu.make_async_copy(fock, fk, load_sem.at[1]),
        pltpu.make_async_copy(owner_at, owner, load_sem.at[2]),
        pltpu.make_async_copy(extents_at, extents, load_sem.at[0]),
    ]
    for copy in loads:
        copy.start()

    peers = around[1:] + [sibling] + x_peer[1:] + z_peer[1:]
    barrier = pltpu.get_barrier_semaphore()
    for peer in peers:
        pl.semaphore_signal(barrier, inc=1, device_id=peer, device_id_type=MESH)
    pl.semaphore_wait(barrier, len(peers))

    def remote(src, dst, send, recv, to):
        return pltpu.make_async_remote_copy(
            src_ref=src, dst_ref=dst, send_sem=send, recv_sem=recv,
            device_id=to, device_id_type=MESH,
        )

    reach = half // 2

    def exchange_up(c):
        return remote(
            amps.at[0, pl.ds(side * mine + c * group, group)],
            from_below.at[pl.ds(c * group, group)],
            ex_up_send.at[c], ex_up_recv.at[c], around[reach],
        )

    def exchange_down(c):
        return remote(
            amps.at[0, pl.ds((1 - side) * mine + c * group, group)],
            from_above.at[pl.ds(c * group, group)],
            ex_down_send.at[c], ex_down_recv.at[c], around[ring - reach],
        )

    for c in range(CHUNKS):
        exchange_up(c).start()
        exchange_down(c).start()

    for copy in loads:
        copy.wait()

    lower_slot = w
    upper_slot = w + plane
    a_low, b_low = owner[0, lower_slot], owner[1, lower_slot]
    a_high, b_high = owner[0, upper_slot], owner[1, upper_slot]
    off = (a_low != b_low).astype(jnp.int32)
    is_low = 1 - side
    below_is_low = lax.div(lax.rem(y + ring - reach, ring), half) == 0
    below_is_low = below_is_low.astype(jnp.int32)
    row = lax.broadcasted_iota(jnp.int32, (width, width), 0)
    col = lax.broadcasted_iota(jnp.int32, (width, width), 1)
    above_diag = jnp.where(row < col, 1, 0)
    below_diag = jnp.where(row > col, 1, 0)
    first_i = jnp.minimum(above_diag + off, 1)
    second_i = below_diag * (1 - off)
    first = first_i > 0
    live = (row < jnp.where(first, extents[a_low], extents[a_high])) & (
        col < jnp.where(first, extents[b_low], extents[b_high])
    )
    plus_below = first_i == below_is_low
    minus_below = second_i == below_is_low

    fock_a1, fock_b1 = fk[a_low], fk[b_low]
    fock_a2, fock_b2 = fk[a_high], fk[b_high]

    acc[...] = jnp.zeros_like(acc)

    def build(p, carry):
        one = from_below[p].astype(jnp.float32)
        two = from_above[p].astype(jnp.float32)
        plus = jnp.where(plus_below, one, two)
        minus = jnp.where(minus_below, one, two)
        xf[pl.ds(p, width, stride=mine), :] = jnp.where(live, plus - minus.T, 0.0)
        return carry

    for c in range(CHUNKS):
        exchange_up(c).wait_recv()
        exchange_down(c).wait_recv()
        lax.fori_loop(c * group, (c + 1) * group, build, 0, unroll=4)

    def up(t, c):
        at = lax.rem(ring - t, ring) if not isinstance(t, int) else (ring - t) % ring
        return remote(
            tiles.at[at, 0, pl.ds(c * span, span)],
            tiles.at[ring - 1 - t, 0, pl.ds(c * span, span)],
            up_send.at[t, c], up_recv.at[t, c], above,
        )

    def down(t, c):
        return remote(
            tiles.at[t, 0, pl.ds(c * span, span)],
            tiles.at[t + 1, 0, pl.ds(c * span, span)],
            down_send.at[t, c], down_recv.at[t, c], below,
        )

    def across(r, c):
        return remote(
            tiles.at[r, 0, pl.ds(c * span, span)],
            tiles.at[r, 1, pl.ds(c * span, span)],
            core_send.at[r, c], core_recv.at[r, c], sibling,
        )

    middle = CHUNKS // 2
    up_order = list(range(CHUNKS))
    down_order = up_order[middle:] + up_order[:middle]
    up_steps = [(t, c) for t in range(half) for c in up_order][: -middle]
    down_steps = [(t, c) for t in range(half) for c in down_order][: -middle]

    def own_chunk(c):
        block = xf[pl.ds(c * span * mine, span * mine), :].astype(jnp.bfloat16)
        tiles[0, 0, pl.ds(c * span, span)] = block.reshape(span, mine, width)

    for i in range(CHUNKS):
        if i < middle:
            own_chunk(up_order[i])
            own_chunk(down_order[i])
        up(*up_steps[i]).start()
        down(*down_steps[i]).start()
    for c in range(CHUNKS):
        across(0, c).start()

    def right_factor(n, r, c):
        block = tiles[r, 0, pl.ds(c * span, span)].reshape(span * mine, width)
        block = block.astype(jnp.float32)
        at_a = lax.div(lax.broadcasted_iota(jnp.int32, block.shape, 0), mine) + c * span
        at_b = lax.broadcasted_iota(jnp.int32, block.shape, 1)
        upper = jnp.where(at_a < at_b, 1, 0) + off > 0
        for m, (keep_here, factor_b) in enumerate(((upper, fock_b1), (at_a > at_b, fock_b2))):
            part = jnp.where(keep_here, block, 0.0).astype(jnp.bfloat16)
            made = dot(part, factor_b, NT).astype(jnp.bfloat16)
            hf[n, m, pl.ds(c * span * mine, span * mine), :] = made.astype(jnp.float32)

    def left_factor(n, to):
        def some(p, carry):
            one = hf[n, 0, pl.ds(p, width, stride=mine), :].astype(jnp.bfloat16)
            two = hf[n, 1, pl.ds(p, width, stride=mine), :].astype(jnp.bfloat16)
            one, two = dot(fock_a1, one, NN), dot(fock_a2, two, NN)
            turned = jnp.where(below_diag > 0, one, two).T
            yf[pl.ds(p, width, stride=mine), :] = jnp.where(first, one, two) - jnp.where(
                off > 0, 0.0, turned
            )
            return carry

        def narrow(c, carry):
            block = yf[pl.ds(c * span * mine, span * mine), :].astype(jnp.bfloat16)
            yb[to, pl.ds(c * span, span)] = block.reshape(span, mine, width)
            return carry

        lax.fori_loop(0, mine, some, 0, unroll=mine)
        lax.fori_loop(0, CHUNKS, narrow, 0)

    unroll = min(32, span)

    def contract(images, slots, to, begin, count):
        def some(i, sums):
            lefts, rights = [], []
            for u in range(unroll):
                a = begin + i * unroll + u
                rights.append(jnp.concatenate([yb[n, a] for n in images], 0))
                lefts.append(
                    jnp.concatenate([tiles[r, k, a] for r in slots for k in (0, 1)], 0)
                )
            return sums + dot(
                jnp.concatenate(lefts, 1), jnp.concatenate(rights, 1), NT
            )

        zero = jnp.zeros((len(slots) * both, len(images) * mine), jnp.float32)
        sums = lax.fori_loop(0, count // unroll, some, zero, unroll=count // unroll)
        for m in range(len(slots)):
            for n in range(len(images)):
                made = sums[m * both : (m + 1) * both, n * mine : (n + 1) * mine]
                acc[pl.ds(to[m][n] * both, both), pl.ds(0, mine)] += made

    def receive(i):
        t, c = up_steps[i]
        up(t, c).wait_recv()
        if i + CHUNKS < len(up_steps):
            up(*up_steps[i + CHUNKS]).start()
        across(ring - 1 - t, c).start()
        t, c = down_steps[i]
        down(t, c).wait_recv()
        if i + CHUNKS < len(down_steps):
            down(*down_steps[i + CHUNKS]).start()
        across(t + 1, c).start()

    def arrived(r, c):
        across(r, c).wait_recv()

    def send_x(d):
        return remote(part_x.at[x], part_x.at[x], x_send.at[d], x_recv.at[x], x_peer[d])

    def wait_x(d):
        return remote(
            part_x.at[x_at[d]], part_x.at[x_at[d]], x_send.at[d], x_recv.at[x_at[d]], x_peer[d]
        )

    def send_z(d):
        return remote(part_z.at[z], part_z.at[z], z_send.at[d], z_recv.at[z], z_peer[d])

    def wait_z(d):
        return remote(
            part_z.at[z_at[d]], part_z.at[z_at[d]], z_send.at[d], z_recv.at[z_at[d]], z_peer[d]
        )

    left_to = (1, 2, ring - 3, ring - 2)
    right_to = (2, 3, half, ring - 2, ring - 1)

    def send_left(d):
        return remote(
            row_left[0], row_left[ring - d], left_send.at[d], left_recv.at[ring - d], around[d]
        )

    def send_right(d):
        return remote(
            row_right[0], row_right[ring - d], right_send.at[d], right_recv.at[ring - d], around[d]
        )

    def row_sends():
        return [send_left(d) for d in left_to] + [send_right(d) for d in right_to]

    last = ring - 1
    for c in range(CHUNKS):
        right_factor(0, 0, c)
    left_factor(0, 0)
    for i in range(CHUNKS):
        receive(i)
        right_factor(0, last, up_order[i])
        right_factor(1, 1, down_order[i])
        arrived(0, i)
        if i == middle:
            contract([0], [0], [[0]], 0, width // 2)
    contract([0], [0], [[0]], width // 2, width // 2)

    halves = (0, width // 2)
    for i in range(CHUNKS):
        receive(CHUNKS + i)
        right_factor(2, last - 1, up_order[i])
        if i == 0:
            for c in range(CHUNKS):
                arrived(1, c)
                arrived(last, c)
        if i < 2:
            left_factor(i, 1 + i)
        if i == 1:
            contract([0], [1, last], [[1], [last]], 0, width)
        if i == 2:
            for j in range(middle):
                arrived(2, down_order[j])
                arrived(last - 1, up_order[j])
            contract([0, 1], [2], [[2, 3]], halves[1], width // 2)
            contract([0, 2], [last - 1], [[last - 1, last - 2]], halves[0], width // 2)
    left_factor(2, 3)
    for j in range(middle, CHUNKS):
        arrived(2, down_order[j])
        arrived(last - 1, up_order[j])
    contract([0, 1], [2], [[2, 3]], halves[0], width // 2)
    contract([0, 2], [last - 1], [[last - 1, last - 2]], halves[1], width // 2)
    contract([3], [2], [[4]], 0, width)

    rows = ring * both
    part_x[x] = jnp.concatenate(
        [acc[pl.ds(n * width, width), :].T[:mine] for n in range(rows // width)], 1
    )
    for d in range(1, nx):
        send_x(d).start()
    receive(2 * CHUNKS)
    receive(2 * CHUNKS + 1)
    for d in range(1, nx):
        wait_x(d).wait_recv()
    total = part_x[0]
    for n in range(1, nx):
        total += part_x[n]
    part_z[z] = total
    for d in range(1, nz):
        send_z(d).start()
    receive(2 * CHUNKS + 2)
    for d in range(1, nz):
        wait_z(d).wait_recv()
    total = part_z[0]
    for n in range(1, nz):
        total += part_z[n]
    nblocks = fk.shape[0]
    made = (total * (2.0 / (nblocks * width))).astype(jnp.bfloat16)
    row_left[0][...] = made[:, : rows // 2]
    row_right[0][...] = made[:, rows // 2 :]
    for copy in row_sends():
        copy.start()
    receive(2 * CHUNKS + 3)
    receive(3 * CHUNKS)
    receive(3 * CHUNKS + 1)
    for copy in row_sends():
        copy.wait_recv()

    place = lax.div(lax.broadcasted_iota(jnp.int32, (mine, rows // 2), 1), both)

    def rows_of(d):
        left = jnp.where(
            place == 3,
            row_left[(d + 1) % ring][...].astype(jnp.float32),
            row_left[d][...].astype(jnp.float32),
        )
        right = jnp.where(
            place == 0,
            row_right[(d + 2) % ring][...].astype(jnp.float32),
            jnp.where(
                place == 1,
                row_right[d - 1][...].astype(jnp.float32),
                row_right[d][...].astype(jnp.float32),
            ),
        )
        return pltpu.roll(jnp.concatenate([left, right], 1), d * both, 1)

    here, there = rows_of(reach), rows_of(ring - reach)
    low = jnp.zeros(here.shape, jnp.int32) + side == 0
    inter = jnp.concatenate(
        [jnp.where(low, here, there), jnp.where(low, there, here)], 0
    ).astype(jnp.bfloat16)
    factor = 1.0 / math.sqrt(rows)
    pair = 2

    def residual(i, carry):
        a = i * pair
        right = jnp.concatenate(
            [tiles[:, :, a + u].reshape(rows, width) for u in range(pair)], 1
        )
        made = dot(inter, right, NN) * factor
        for u in range(pair):
            zs[pl.ds((a + u) * both, both), :] = made[:, u * width : (u + 1) * width]
        return carry

    for i in range(middle):
        for c in (up_order[i], down_order[i]):
            for r in range(3, ring - 2):
                arrived(r, c)
            lax.fori_loop(c * span // pair, (c + 1) * span // pair, residual, 0, unroll=16)

    triangle = is_low * above_diag + side * below_diag
    keep = (off * is_low + (1 - off) * triangle) > 0

    def unpack(p, carry):
        tile = zs[pl.ds(p, width, stride=both), :]
        out[0, p] = jnp.where(keep, tile, -tile.T).astype(jnp.bfloat16)
        return carry

    lax.fori_loop(0, both, unpack, 0, unroll=8)

    for c in range(CHUNKS):
        exchange_up(c).wait_send()
        exchange_down(c).wait_send()
        for r in range(ring):
            across(r, c).wait_send()
    for i in range(len(up_steps)):
        up(*up_steps[i]).wait_send()
        down(*down_steps[i]).wait_send()
    for d in range(1, nx):
        send_x(d).wait_send()
    for d in range(1, nz):
        send_z(d).wait_send()
    for copy in row_sends():
        copy.wait_send()


def body(sizes, amplitudes, fock_blocks, owner_map, extents):
    ring, nz, nx = sizes
    slots, both, width = amplitudes.shape[0], amplitudes.shape[1], amplitudes.shape[2]
    mine = both // 2
    half = ring // 2
    rows = ring * both
    dma = pltpu.SemaphoreType.DMA
    hbm = pl.BlockSpec(memory_space=pltpu.HBM)
    bf16, f32 = jnp.bfloat16, jnp.float32
    return pl.pallas_call(
        functools.partial(kernel, sizes),
        out_shape=jax.ShapeDtypeStruct((slots, both, width, width), bf16),
        in_specs=[hbm, hbm, hbm, hbm],
        out_specs=pl.BlockSpec(memory_space=pltpu.VMEM),
        scratch_shapes=[
            pltpu.SMEM(owner_map.shape[::-1], jnp.int32),
            pltpu.SMEM(extents.shape, jnp.int32),
            pltpu.VMEM((mine, width, width), bf16),
            pltpu.VMEM((mine, width, width), bf16),
            pltpu.VMEM(fock_blocks.shape, bf16),
            pltpu.VMEM((width * mine + mine, width), f32),
            pltpu.VMEM((width * mine + mine, width), f32),
            pltpu.VMEM((3, 2, width * mine + mine, width), f32),
            pltpu.VMEM((4, width, mine, width), bf16),
            pltpu.VMEM((ring, 2, width, mine, width), bf16),
            pltpu.VMEM((rows, width), f32),
            pltpu.VMEM((nx, mine, rows), f32),
            pltpu.VMEM((nz, mine, rows), f32),
            [pltpu.VMEM((mine, rows // 2), bf16)] * ring,
            [pltpu.VMEM((mine, rows // 2), bf16)] * ring,
            pltpu.VMEM((width * both + both, width), f32),
            dma((3,)),
            dma((CHUNKS,)), dma((CHUNKS,)), dma((CHUNKS,)), dma((CHUNKS,)),
            dma((half, CHUNKS)), dma((half, CHUNKS)),
            dma((half, CHUNKS)), dma((half, CHUNKS)),
            dma((ring, CHUNKS)), dma((ring, CHUNKS)),
            dma((nx,)), dma((nx,)),
            dma((nz,)), dma((nz,)),
            dma((ring,)), dma((ring,)), dma((ring,)), dma((ring,)),
        ],
        compiler_params=pltpu.CompilerParams(
            collective_id=0, has_side_effects=True, vmem_limit_bytes=48 * 1024 * 1024
        ),
        cost_estimate=pl.CostEstimate(
            flops=2**30, bytes_accessed=2**22, transcendentals=0
        ),
    )(*[
        pltpu.with_memory_space_constraint(value, pltpu.HBM)
        for value in (amplitudes, fock_blocks, owner_map.T, extents)
    ])


def solution(mesh):
    plane = mesh.shape["vpair"] // 2
    nx = 4 if plane % 4 == 0 else 1
    sizes = (mesh.shape["occ"], plane // nx, nx)
    placed = (P("vpair", "occ", None, None), P(), P(), P())
    return jax.shard_map(
        functools.partial(body, sizes),
        mesh=mesh,
        in_specs=placed,
        out_specs=P("vpair", "occ", None, None),
        check_vma=False,
    )
```
